512 devices in a mesh: seg: 8 (over x, core), sec: 64 (over z, y).
Axes of the slice: x: 4, y: 4, z: 16, core: 2. Of those that a mesh axis runs over, the one named last changes fastest.
Arguments:
- site_tensors: bfloat16 [8, 64, 4, 128, 128], P('seg', 'sec'), may hold values from -0.5 to 0.5
- boundary: bfloat16 [8, 64, 24, 128, 128], P('seg', 'sec'), may hold values from -6 to 6
- couplings: float32 [8, 4, 24, 24], P('seg'), may hold values from -0.9 to 0.9
- pattern: int32 [24, 24], replicated, may hold values 0 or 1
- block_sizes: int32 [64], replicated, may hold values from 64 to 128, as said below
Outputs:
- environments: bfloat16 [8, 64, 24, 128, 128], P('seg', 'sec')
- handoff: bfloat16 [8, 64, 24, 128, 128], P('seg', 'sec')
The draws below stay inside these ranges and needn't reach their ends.
Inputs may be any that keep to these rules, and one draw needn't show every extreme that they name: `block_sizes`: each sector has between half and all of 128 live rows, and some sector has all 128.
All inputs are finite; a program needn't handle non-finite values.
Results may differ from the reference program's by a relative error of at most 0.0049.
Values may be sent and summed in bfloat16 or wider, within the bound.
No kernel may reach another device: no remote copies, remote signals or barrier semaphores. Data moves between devices by JAX's collectives and lax.ppermute only.
A program may use at most 64 MiB of HBM per device.

```python
import jax
import jax.numpy as jnp
from jax import lax

BLOCK = 128
CHANNELS = 24
STATES = 4
CHARGES = 8
SITES = 1
SECTORS = 64
SEGMENTS = 8
WINDOW = 8


def draw_block_sizes(key, part):
    first_key, second_key = jax.random.split(key)
    values = jax.random.randint(first_key, (SECTORS,), BLOCK // 2, BLOCK + 1)
    chosen = jax.random.randint(second_key, (), 0, SECTORS)
    return jnp.where(jnp.arange(SECTORS) == chosen, BLOCK, values).astype(jnp.int32)


def with_ends(entries, rng, smallest, high):
    extent = entries.shape
    spot = [jax.random.randint(jax.random.fold_in(rng, axis), (), 0, extent[axis]) for axis in range(len(extent))]
    entries = entries.at[tuple(spot)].set(smallest)
    longest = extent.index(max(extent))
    spot[longest] = (spot[longest] + 1) % extent[longest]
    return entries.at[tuple(spot)].set(high)


def shard_levels(own_key, extent, cuts, smallest, top_value):
    factor_of = 1.0
    for axis_at, blocks in cuts:
        steps = jax.random.uniform(jax.random.fold_in(jax.random.fold_in(own_key, 6), axis_at), (blocks,), jnp.float32, smallest / len(cuts), top_value / len(cuts))
        factor_of = factor_of * jnp.repeat(jnp.exp(steps), extent[axis_at] // blocks).reshape((-1,) + (1,) * (len(extent) - 1 - axis_at))
    return factor_of


def bell_draw(stream_key, shape, deviation, reach, shards=(), held_as=jnp.bfloat16):
    gain = shard_levels(stream_key, shape, shards, -0.22, 0.18) if shards else 1.0
    array = jax.random.normal(stream_key, shape, jnp.float32) * deviation * gain
    return jnp.minimum(jnp.maximum(array, -reach), reach).astype(held_as)


def setup_inputs(seed: int = 0) -> dict:
    key_list = jax.random.split(jax.random.key(seed), 6)
    site_tensors = bell_draw(key_list[0], (WINDOW, SECTORS, STATES, BLOCK, BLOCK), BLOCK ** -0.5, 0.5, ((0, 8), (1, 64)))
    boundary = bell_draw(key_list[1], (SEGMENTS, SECTORS, CHANNELS, BLOCK, BLOCK), 1.0, 6.0, ((0, 8), (1, 64)))
    couplings = bell_draw(key_list[2], (WINDOW, STATES, CHANNELS, CHANNELS), 0.15, 0.9, ((0, 8),), jnp.float32)
    pattern = with_ends((jax.random.randint(key_list[3], (CHANNELS, CHANNELS), 0, 2) < 1).astype(jnp.int32), jax.random.fold_in(key_list[3], 1), 0, 1)
    block_sizes = draw_block_sizes(jax.random.fold_in(key_list[5], 71), 0)
    return dict(site_tensors=site_tensors, boundary=boundary, couplings=couplings, pattern=pattern, block_sizes=block_sizes)


def masked_blocks(blocks, sizes_rows, sizes_cols):
    row_index = jnp.arange(BLOCK)
    kept_rows = row_index[None, :] < sizes_rows[:, None]
    kept_cols = row_index[None, :] < sizes_cols[:, None]
    kept_mask = kept_rows[:, :, None] & kept_cols[:, None, :]
    return blocks * kept_mask.astype(jnp.bfloat16)


def site_update(current, tensors, weights, pattern, block_sizes):
    sector = jnp.arange(SECTORS).astype(jnp.int32)
    down_charge = sector % CHARGES
    accumulated = jnp.zeros((SECTORS, CHANNELS, BLOCK, BLOCK), jnp.float32)
    for state_index in range(STATES):
        up_count = state_index // 2
        down_count = state_index % 2
        offset = up_count * CHARGES + down_count
        source = sector - offset
        usable = (source >= 0) & (down_charge >= down_count)
        clipped = jnp.clip(source, 0, SECTORS - 1).astype(jnp.int32)
        blocks = masked_blocks(tensors[clipped, state_index], block_sizes[clipped], block_sizes)
        inputs = current[clipped]
        halfway = jnp.einsum("qbik,qkl->qbil", inputs.astype(jnp.float32), blocks.astype(jnp.float32)).astype(jnp.bfloat16)
        sandwich = jnp.einsum("qki,qbkl->qbil", blocks.astype(jnp.float32), halfway.astype(jnp.float32))
        mixing = weights[state_index] * pattern.astype(jnp.float32)
        contribution = jnp.einsum("bc,qbil->qcil", mixing, sandwich, precision=lax.Precision.HIGHEST)
        accumulated = accumulated + jnp.where(usable[:, None, None, None], contribution, jnp.float32(0.0))
    return accumulated.astype(jnp.bfloat16)


def reference(site_tensors, boundary, couplings, pattern, block_sizes):
    results = []
    handed = [jnp.zeros((SECTORS, CHANNELS, BLOCK, BLOCK), jnp.bfloat16)]
    for segment in range(SEGMENTS):
        current = boundary[segment]
        for site_index in range(SITES):
            position = segment * SITES + site_index
            current = site_update(current, site_tensors[position], couplings[position], pattern, block_sizes)
            results.append(current)
        if segment + 1 < SEGMENTS:
            handed.append(current)
    return jnp.stack(results), jnp.stack(handed)
```

```python
import functools

import jax
import jax.numpy as jnp
from jax import lax
from jax.experimental import pallas as pl
from jax.experimental.pallas import tpu as pltpu
from jax.sharding import PartitionSpec as P

STATES = 4
CHARGES = 8
BLOCK = 128
CHANNELS = 24
SECTORS = 64
TILE = 16
ROWS = CHANNELS * TILE
SPLITS = ((0, 12), (12, 24))

VMEM = pl.BlockSpec(memory_space=pltpu.VMEM)
SMEM = pl.BlockSpec(memory_space=pltpu.SMEM)


def passed_along(shard, axis, by):
    devices = lax.axis_size(axis)
    pairs = [(i, i + by) for i in range(devices) if 0 <= i + by < devices]
    if axis == "sec" and by == 1:
        pairs = [(i, j) for i, j in pairs if j % CHARGES]
    return lax.ppermute(shard, axis, pairs)


def two_terms(x):
    high = x.astype(jnp.bfloat16)
    low = (x - high.astype(jnp.float32)).astype(jnp.bfloat16)
    return high, low


def spread_weights(weights):
    row_channel = lax.broadcasted_iota(jnp.int32, (ROWS, CHANNELS), 0) // TILE
    channel = lax.broadcasted_iota(jnp.int32, (ROWS, CHANNELS), 1)
    onehot = (row_channel == channel).astype(jnp.bfloat16)
    row = lax.broadcasted_iota(jnp.int32, (ROWS, ROWS), 0) % TILE
    col = lax.broadcasted_iota(jnp.int32, (ROWS, ROWS), 1) % TILE
    same = row == col
    parts = []
    for term in two_terms(weights):
        by_row = lax.dot_general(onehot, term, (((1,), (1,)), ((), ())), preferred_element_type=jnp.float32)
        full = lax.dot_general(
            by_row.astype(jnp.bfloat16), onehot, (((1,), (1,)), ((), ())), preferred_element_type=jnp.float32
        )
        parts.append(jnp.where(same, full, 0.0).astype(jnp.bfloat16))
    return jnp.concatenate(parts, axis=1)


def masked(block, rows, cols):
    row = lax.broadcasted_iota(jnp.int32, (BLOCK, BLOCK), 0)
    col = lax.broadcasted_iota(jnp.int32, (BLOCK, BLOCK), 1)
    return jnp.where((row < rows) & (col < cols), block.astype(jnp.float32), 0.0)


def update(cur_ref, block, spread, count, mixed_ref, emit):
    for pair in range(BLOCK // (2 * TILE)):
        first = pair * 2 * TILE
        left = cur_ref[:, first : first + TILE, :].reshape(ROWS, BLOCK)
        right = cur_ref[:, first + TILE : first + 2 * TILE, :].reshape(ROWS, BLOCK)
        both = jnp.concatenate([left, right], axis=1)
        both = jnp.concatenate([both, both], axis=0)
        mixed = jnp.dot(spread, both, preferred_element_type=jnp.float32)
        for half in range(2):
            at = first + half * TILE
            part = mixed[:, half * BLOCK : (half + 1) * BLOCK].reshape(count, TILE, BLOCK)
            high, low = two_terms(part)
            mixed_ref[:count, at : at + TILE, :BLOCK] = high
            mixed_ref[:count, at : at + TILE, BLOCK:] = low
    stacked = block.astype(jnp.bfloat16)
    stacked = jnp.concatenate([stacked, stacked], axis=0)
    turned = block.T.astype(jnp.bfloat16)
    turned = jnp.concatenate([turned, turned], axis=1)
    for c in range(0, count, 2):
        rows = mixed_ref[c : c + 2].reshape(2 * BLOCK, 2 * BLOCK)
        half = jnp.dot(rows, stacked, preferred_element_type=jnp.float32)
        high, low = two_terms(half)
        first = jnp.concatenate([high[:BLOCK], high[BLOCK:]], axis=1)
        second = jnp.concatenate([low[:BLOCK], low[BLOCK:]], axis=1)
        pairs = jnp.concatenate([first, second], axis=0)
        result = jnp.dot(turned, pairs, preferred_element_type=jnp.float32)
        emit(c, result[:, :BLOCK], result[:, BLOCK:])


def sizes_of(sizes_ref, position):
    return sizes_ref[jnp.clip(position, 0, SECTORS - 1)]


def weights_of(couplings_ref, pattern_ref, state):
    return couplings_ref[state] * pattern_ref[...].astype(jnp.float32)


def own_kernel(sizes_ref, cur_ref, tensors_ref, couplings_ref, pattern_ref, keep_ref, pass_ref, spread_ref, mixed_ref):
    sector = lax.axis_index("sec")
    rows = sizes_of(sizes_ref, sector)
    for state, out in ((2, pass_ref), (0, keep_ref)):
        cols = sizes_of(sizes_ref, sector + state // 2 * CHARGES)
        block = masked(tensors_ref[state], rows, cols)
        spread = spread_weights(weights_of(couplings_ref, pattern_ref, state))

        def emit(c, first, second, out=out):
            out[c] = first
            out[c + 1] = second

        update(cur_ref, block, spread, CHANNELS, mixed_ref, emit)
    for at, state in enumerate((1, 3)):
        spread_ref[at] = spread_weights(weights_of(couplings_ref, pattern_ref, state))


def moved_kernel(state, low, high, sizes_ref, cur_ref, tensors_ref, spread_ref, base_ref, out_ref, mixed_ref):
    sector = lax.axis_index("sec")
    rows = sizes_of(sizes_ref, sector - 1)
    cols = sizes_of(sizes_ref, sector + state // 2 * CHARGES)
    block = masked(tensors_ref[state // 2], rows, cols)
    spread = spread_ref[state // 2, low * TILE : high * TILE, :]

    def emit(c, first, second):
        out_ref[c] = (base_ref[low + c] + first).astype(out_ref.dtype)
        out_ref[c + 1] = (base_ref[low + c + 1] + second).astype(out_ref.dtype)

    update(cur_ref, block, spread, high - low, mixed_ref, emit)


def scratch(count):
    return [pltpu.VMEM((count, BLOCK, 2 * BLOCK), jnp.bfloat16)]


PARAMS = pltpu.CompilerParams(vmem_limit_bytes=32 * 1024 * 1024)


def own(sizes, cur, tensors, couplings, pattern):
    full = jax.ShapeDtypeStruct((CHANNELS, BLOCK, BLOCK), jnp.float32)
    return pl.pallas_call(
        own_kernel,
        out_shape=(full, full, jax.ShapeDtypeStruct((2, ROWS, 2 * ROWS), jnp.bfloat16)),
        in_specs=[SMEM, VMEM, VMEM, VMEM, VMEM],
        out_specs=(VMEM, VMEM, VMEM),
        scratch_shapes=scratch(CHANNELS),
        compiler_params=PARAMS,
        name="own",
    )(sizes, cur, tensors, couplings, pattern)


def moved(state, low, high, dtype, sizes, cur, tensors, spread, base):
    return pl.pallas_call(
        functools.partial(moved_kernel, state, low, high),
        out_shape=jax.ShapeDtypeStruct((high - low, BLOCK, BLOCK), dtype),
        in_specs=[SMEM, VMEM, VMEM, VMEM, VMEM],
        out_specs=VMEM,
        scratch_shapes=scratch(high - low),
        compiler_params=PARAMS,
        name=f"moved_{state}_{low}",
    )(sizes, cur, tensors, spread, base)


def total_kernel(low, high, kept_ref, part_ref, out_ref):
    out_ref[...] = (kept_ref[low:high] + part_ref[...].astype(jnp.float32)).astype(jnp.bfloat16)


def total(low, high, kept, part):
    return pl.pallas_call(
        functools.partial(total_kernel, low, high),
        out_shape=jax.ShapeDtypeStruct(part.shape, jnp.bfloat16),
        in_specs=[VMEM, VMEM],
        out_specs=VMEM,
        compiler_params=PARAMS,
        name=f"total_{low}",
    )(kept, part)


def per_device(site_tensors, boundary, couplings, pattern, block_sizes):
    cur = boundary[0, 0]
    tensors = site_tensors[0, 0]
    cur_before = passed_along(cur, "sec", 1)
    tensors_before = passed_along(tensors[1::2], "sec", 1)
    kept, passing, spread = own(block_sizes, cur, tensors, couplings[0], pattern)
    arrived = []
    for low, high in SPLITS:
        sent = moved(3, low, high, jnp.bfloat16, block_sizes, cur_before, tensors_before, spread, passing)
        arrived.append(passed_along(sent, "sec", CHARGES))
    kept = moved(1, 0, CHANNELS, jnp.float32, block_sizes, cur_before, tensors_before, spread, kept)
    done, handed = [], []
    for (low, high), part in zip(SPLITS, arrived):
        result = total(low, high, kept, part)
        done.append(result)
        handed.append(passed_along(result, "seg", 1))
    return jnp.concatenate(done)[None, None], jnp.concatenate(handed)[None, None]


def solution(mesh):
    return jax.shard_map(
        per_device,
        mesh=mesh,
        in_specs=(
            P("seg", "sec", None, None, None),
            P("seg", "sec", None, None, None),
            P("seg", None, None, None),
            P(),
            P(),
        ),
        out_specs=(P("seg", "sec", None, None, None), P("seg", "sec", None, None, None)),
        check_vma=False,
    )
```

```python
import functools

import jax
import jax.numpy as jnp
from jax import lax
from jax.experimental import pallas as pl
from jax.experimental.pallas import tpu as pltpu
from jax.sharding import PartitionSpec as P

STATES = 4
CHARGES = 8
BLOCK = 128
CHANNELS = 24
SECTORS = 64
TILE = 16
ROWS = CHANNELS * TILE
CUTS = (0, 6, 12, 18, 24)
CHUNKS = tuple(zip(CUTS[:-1], CUTS[1:]))
VMEM = pl.BlockSpec(memory_space=pltpu.VMEM)
SMEM = pl.BlockSpec(memory_space=pltpu.SMEM)
HBM = pl.BlockSpec(memory_space=pltpu.HBM)
ANY = pl.BlockSpec(memory_space=pl.ANY)
PARAMS = pltpu.CompilerParams(vmem_limit_bytes=32 * 1024 * 1024)
MIXED = pltpu.VMEM((CHANNELS, BLOCK, BLOCK), jnp.bfloat16)


def array(dtype, *shape):
    return jax.ShapeDtypeStruct(shape, dtype)


def send(shard, axis, by):
    devices = lax.axis_size(axis)
    pairs = [(i, i + by) for i in range(devices) if 0 <= i + by < devices]
    if axis == "sec" and by == 1:
        pairs = [(i, j) for i, j in pairs if j % CHARGES]
    return lax.ppermute(shard, axis, pairs)


def two_terms(x):
    high = x.astype(jnp.bfloat16)
    low = (x - high.astype(jnp.float32)).astype(jnp.bfloat16)
    return high, low


def spread_weights(weights, low, high):
    rows = (high - low) * TILE
    channel_of_row = lax.broadcasted_iota(jnp.int32, (rows, CHANNELS), 0) // TILE + low
    pick_c = (channel_of_row == lax.broadcasted_iota(jnp.int32, (rows, CHANNELS), 1)).astype(jnp.bfloat16)
    channel_of_row = lax.broadcasted_iota(jnp.int32, (ROWS, CHANNELS), 0) // TILE
    pick_b = (channel_of_row == lax.broadcasted_iota(jnp.int32, (ROWS, CHANNELS), 1)).astype(jnp.bfloat16)
    row = lax.broadcasted_iota(jnp.int32, (rows, ROWS), 0) % TILE
    col = lax.broadcasted_iota(jnp.int32, (rows, ROWS), 1) % TILE
    same = row == col
    contract = (((1,), (1,)), ((), ()))
    parts = []
    for term in two_terms(weights):
        by_row = lax.dot_general(pick_c, term, contract, preferred_element_type=jnp.float32)
        full = lax.dot_general(by_row.astype(jnp.bfloat16), pick_b, contract, preferred_element_type=jnp.float32)
        parts.append(jnp.where(same, full, 0.0).astype(jnp.bfloat16))
    return jnp.concatenate(parts, axis=1)


def update(cur_ref, block, spread, count, mixed_ref, emit):
    for first in range(0, BLOCK, 2 * TILE):
        left = cur_ref[:CHANNELS, first : first + TILE, :].reshape(ROWS, BLOCK)
        right = cur_ref[:CHANNELS, first + TILE : first + 2 * TILE, :].reshape(ROWS, BLOCK)
        both = jnp.concatenate([left, right], axis=1)
        both = jnp.concatenate([both, both], axis=0)
        mixed = jnp.dot(spread, both, preferred_element_type=jnp.float32).astype(jnp.bfloat16)
        for half in range(2):
            at = first + half * TILE
            mixed_ref[:count, at : at + TILE, :] = mixed[:, half * BLOCK : (half + 1) * BLOCK].reshape(count, TILE, BLOCK)
    left_block = block.astype(jnp.float32).T.astype(jnp.bfloat16)
    left_block = jnp.concatenate([left_block, left_block], axis=1)
    for c in range(0, count, 2):
        rows = mixed_ref[c : c + 2].reshape(2 * BLOCK, BLOCK)
        high, low = two_terms(jnp.dot(rows, block, preferred_element_type=jnp.float32))
        first = jnp.concatenate([high[:BLOCK], high[BLOCK:]], axis=1)
        second = jnp.concatenate([low[:BLOCK], low[BLOCK:]], axis=1)
        pairs = jnp.concatenate([first, second], axis=0)
        result = jnp.dot(left_block, pairs, preferred_element_type=jnp.float32)
        emit(c, result[:, :BLOCK])
        emit(c + 1, result[:, BLOCK:])


def masked(block, rows, cols):
    row = lax.broadcasted_iota(jnp.int32, (BLOCK, BLOCK), 0)
    col = lax.broadcasted_iota(jnp.int32, (BLOCK, BLOCK), 1)
    return jnp.where((row < rows) & (col < cols), block.astype(jnp.float32), 0.0).astype(jnp.bfloat16)


def loaded_kernel(sizes_hbm, cur_hbm, tensors_hbm, couplings_hbm, pattern_hbm, *refs):
    cur_ref, even_ref, odd_ref, weights_ref, sizes_ref, tensors_ref, pattern_ref, sems = refs
    copies = [
        pltpu.make_async_copy(source, target, sems.at[at])
        for at, (source, target) in enumerate(
            (
                (sizes_hbm, sizes_ref),
                (tensors_hbm, tensors_ref),
                (couplings_hbm, weights_ref),
                (pattern_hbm, pattern_ref),
                (cur_hbm, cur_ref),
            )
        )
    ]
    for copy in copies:
        copy.start()
    copies[0].wait()
    copies[1].wait()
    sector = lax.axis_index("sec")
    for state in range(STATES):
        target = jnp.minimum(sector + state // 2 * CHARGES + state % 2, SECTORS - 1)
        kept_ref = odd_ref if state % 2 else even_ref
        kept_ref[state // 2] = masked(tensors_ref[state], sizes_ref[sector], sizes_ref[target])
    copies[2].wait()
    copies[3].wait()
    pattern = pattern_ref[...].astype(jnp.float32)
    for state in range(STATES):
        weights_ref[state] = weights_ref[state] * pattern
    copies[4].wait()


COSTS = dict(
    loaded=1, own_2=1, own_0=1, kept=1,
    **{f"{kind}_{low}": 1 if kind == "sent" or low == CUTS[-2] else 10 for kind in ("sent", "total", "placed") for low in CUTS},
)


def cost(name):
    return pl.CostEstimate(flops=int(COSTS[name] * 2.5e9), bytes_accessed=1 << 20, transcendentals=0)


def loaded(sizes, cur, tensors, couplings, pattern):
    stay = [pltpu.with_memory_space_constraint(x, pltpu.HBM) for x in (sizes, cur, tensors, couplings, pattern)]
    return pl.pallas_call(
        loaded_kernel,
        out_shape=(
            array(jnp.bfloat16, CHANNELS, BLOCK, BLOCK),
            array(jnp.bfloat16, 2, BLOCK, BLOCK),
            array(jnp.bfloat16, 2, BLOCK, BLOCK),
            array(jnp.float32, STATES, CHANNELS, CHANNELS),
        ),
        in_specs=[HBM] * 5,
        out_specs=(VMEM,) * 4,
        scratch_shapes=[
            pltpu.SMEM((SECTORS,), jnp.int32),
            pltpu.VMEM((STATES, BLOCK, BLOCK), jnp.bfloat16),
            pltpu.VMEM((CHANNELS, CHANNELS), jnp.int32),
            pltpu.SemaphoreType.DMA((5,)),
        ],
        compiler_params=PARAMS,
        cost_estimate=cost("loaded"),
        name="loaded",
    )(*stay)


def own_kernel(state, cur_ref, even_ref, weights_ref, _, out_ref, spread_ref, mixed_ref):
    def emit(c, value):
        out_ref[c] = value

    spread = spread_weights(weights_ref[state], 0, CHANNELS)
    update(cur_ref, even_ref[state // 2], spread, CHANNELS, mixed_ref, emit)
    spread_ref[...] = spread_weights(weights_ref[state + 1], 0, CHANNELS)


def own(state, cur, even, weights, after):
    name = f"own_{state}"
    return pl.pallas_call(
        functools.partial(own_kernel, state),
        out_shape=(array(jnp.float32, CHANNELS, BLOCK, BLOCK), array(jnp.bfloat16, ROWS, 2 * ROWS)),
        in_specs=[VMEM] * 3 + [ANY],
        out_specs=(VMEM,) * 2,
        scratch_shapes=[MIXED],
        compiler_params=PARAMS,
        cost_estimate=cost(name),
        name=name,
    )(cur, even, weights, after)


def joined_kernel(state, low, high, base_ref, spread_ref, raw_ref, odd_ref, _, out_ref, mixed_ref):
    def emit(c, value):
        out_ref[c] = (base_ref[low + c] + value).astype(out_ref.dtype)

    spread = spread_ref[low * TILE : high * TILE, :]
    update(raw_ref, odd_ref[state // 2], spread, high - low, mixed_ref, emit)


def joined(name, state, low, high, dtype, base, spread, raw, odd, after):
    return pl.pallas_call(
        functools.partial(joined_kernel, state, low, high),
        out_shape=array(dtype, high - low, BLOCK, BLOCK),
        in_specs=[VMEM] * 4 + [ANY],
        out_specs=VMEM,
        scratch_shapes=[MIXED],
        compiler_params=PARAMS,
        cost_estimate=cost(name),
        name=name,
    )(base, spread, raw, odd, after)


def total_kernel(low, high, base_ref, up_ref, _, out_ref):
    out_ref[...] = (
        base_ref[low:high] + up_ref[...].astype(jnp.float32)
    ).astype(jnp.bfloat16)


def whole_of(part):
    return array(part.dtype, CHANNELS, BLOCK, BLOCK)


def total(low, high, base, up, after):
    return pl.pallas_call(
        functools.partial(total_kernel, low, high),
        out_shape=array(jnp.bfloat16, high - low, BLOCK, BLOCK),
        in_specs=[VMEM, VMEM, ANY],
        out_specs=VMEM,
        compiler_params=PARAMS,
        cost_estimate=cost(f"total_{low}"),
        name=f"total_{low}",
    )(base, up, after)


def placed_kernel(low, high, part_ref, *refs):
    whole_hbm, sem = refs[-2:]
    copy = pltpu.make_async_copy(part_ref, whole_hbm.at[low:high], sem)
    copy.start()
    copy.wait()


def placed(low, high, part, whole):
    given = [] if whole is None else [whole]
    return pl.pallas_call(
        functools.partial(placed_kernel, low, high),
        out_shape=whole_of(part),
        in_specs=[VMEM] + [HBM] * len(given),
        out_specs=HBM,
        scratch_shapes=[pltpu.SemaphoreType.DMA],
        input_output_aliases={1: 0} if given else {},
        compiler_params=PARAMS,
        cost_estimate=cost(f"placed_{low}"),
        name=f"placed_{low}",
    )(part, *given)


def per_device(site_tensors, boundary, couplings, pattern, sizes):
    raw = send(boundary[0, 0], "sec", 1)
    cur, even, odd, weights = loaded(sizes, boundary[0, 0], site_tensors[0, 0], couplings[0], pattern)
    odd = send(odd, "sec", 1)
    up, spread_up = own(2, cur, even, weights, weights)
    kept, spread_kept = own(0, cur, even, weights, up)
    arrived, done, handed = [], [], None
    last = kept

    def go_up(last):
        low, high = CHUNKS[len(arrived)]
        last = joined(f"sent_{low}", 3, low, high, jnp.bfloat16, up, spread_up, raw, odd, last)
        arrived.append(send(last, "sec", CHARGES))
        return last

    for _ in range(3):
        last = go_up(last)
    kept = last = joined("kept", 1, 0, CHANNELS, jnp.float32, kept, spread_kept, raw, odd, last)
    for at, (low, high) in enumerate(CHUNKS):
        last = total(low, high, kept, arrived[at], last)
        done.append(last)
        handed = placed(low, high, send(last, "seg", 1), handed)
        if len(arrived) < len(CHUNKS):
            last = go_up(last)
    return jnp.concatenate(done)[None, None], handed[None, None]


def solution(mesh):
    return jax.shard_map(
        per_device,
        mesh=mesh,
        in_specs=(
            P("seg", "sec", None, None, None),
            P("seg", "sec", None, None, None),
            P("seg", None, None, None),
            P(),
            P(),
        ),
        out_specs=(P("seg", "sec", None, None, None), P("seg", "sec", None, None, None)),
        check_vma=False,
    )
```

```python
import functools

import jax
import jax.numpy as jnp
from jax import lax
from jax.experimental import pallas as pl
from jax.experimental.pallas import tpu as pltpu
from jax.sharding import PartitionSpec as P

STATES = 4
CHARGES = 8
BLOCK = 128
CHANNELS = 24
SECTORS = 64
TILE = 16
ROWS = CHANNELS * TILE
CARRY = 3
PLAIN = (0, 1, 2, 4, 5, 6)
HEAD = 18
TAIL = CHANNELS - HEAD
CUTS = (0, 12, 24)
HANDED = ((0,), (1,))
CHUNKS = tuple(zip(CUTS[:-1], CUTS[1:]))
VMEM = pl.BlockSpec(memory_space=pltpu.VMEM)
SMEM = pl.BlockSpec(memory_space=pltpu.SMEM)
HBM = pl.BlockSpec(memory_space=pltpu.HBM)
ANY = pl.BlockSpec(memory_space=pl.ANY)
PARAMS = pltpu.CompilerParams(vmem_limit_bytes=32 * 1024 * 1024)
MIXED = pltpu.VMEM((CHANNELS, BLOCK, BLOCK), jnp.bfloat16)


def array(dtype, *shape):
    return jax.ShapeDtypeStruct(shape, dtype)


def send(shard, axis, by, charges=range(CHARGES)):
    devices = lax.axis_size(axis)
    pairs = [(i, i + by) for i in range(devices) if 0 <= i + by < devices]
    if axis == "sec":
        pairs = [(i, j) for i, j in pairs if i % CHARGES in charges]
    return lax.ppermute(shard, axis, pairs)


def two_terms(x):
    high = x.astype(jnp.bfloat16)
    low = (x - high.astype(jnp.float32)).astype(jnp.bfloat16)
    return high, low


def spread_weights(weights, low, high):
    rows = (high - low) * TILE
    channel_of_row = lax.broadcasted_iota(jnp.int32, (rows, CHANNELS), 0) // TILE + low
    pick_c = (channel_of_row == lax.broadcasted_iota(jnp.int32, (rows, CHANNELS), 1)).astype(jnp.bfloat16)
    channel_of_row = lax.broadcasted_iota(jnp.int32, (ROWS, CHANNELS), 0) // TILE
    pick_b = (channel_of_row == lax.broadcasted_iota(jnp.int32, (ROWS, CHANNELS), 1)).astype(jnp.bfloat16)
    row = lax.broadcasted_iota(jnp.int32, (rows, ROWS), 0) % TILE
    col = lax.broadcasted_iota(jnp.int32, (rows, ROWS), 1) % TILE
    same = row == col
    contract = (((1,), (1,)), ((), ()))
    parts = []
    for term in two_terms(weights):
        by_row = lax.dot_general(pick_c, term, contract, preferred_element_type=jnp.float32)
        full = lax.dot_general(by_row.astype(jnp.bfloat16), pick_b, contract, preferred_element_type=jnp.float32)
        parts.append(jnp.where(same, full, 0.0).astype(jnp.bfloat16))
    return jnp.concatenate(parts, axis=1)


def update(cur_refs, block, spread, count, mixed_ref, emit):
    def rows_at(at):
        parts = [ref[:, at : at + TILE, :].reshape(ref.shape[0] * TILE, BLOCK) for ref in cur_refs]
        return parts[0] if len(parts) == 1 else jnp.concatenate(parts, axis=0)

    for first in range(0, BLOCK, 2 * TILE):
        left, right = rows_at(first), rows_at(first + TILE)
        both = jnp.concatenate([left, right], axis=1)
        both = jnp.concatenate([both, both], axis=0)
        mixed = jnp.dot(spread, both, preferred_element_type=jnp.float32).astype(jnp.bfloat16)
        for half in range(2):
            at = first + half * TILE
            mixed_ref[:count, at : at + TILE, :] = mixed[:, half * BLOCK : (half + 1) * BLOCK].reshape(count, TILE, BLOCK)
    left_block = block.astype(jnp.float32).T.astype(jnp.bfloat16)
    left_block = jnp.concatenate([left_block, left_block], axis=1)
    for c in range(0, count, 2):
        rows = mixed_ref[c : c + 2].reshape(2 * BLOCK, BLOCK)
        high, low = two_terms(jnp.dot(rows, block, preferred_element_type=jnp.float32))
        first = jnp.concatenate([high[:BLOCK], high[BLOCK:]], axis=1)
        second = jnp.concatenate([low[:BLOCK], low[BLOCK:]], axis=1)
        pairs = jnp.concatenate([first, second], axis=0)
        result = jnp.dot(left_block, pairs, preferred_element_type=jnp.float32)
        emit(c, result[:, :BLOCK])
        emit(c + 1, result[:, BLOCK:])


def masked(block, rows, cols):
    row = lax.broadcasted_iota(jnp.int32, (BLOCK, BLOCK), 0)
    col = lax.broadcasted_iota(jnp.int32, (BLOCK, BLOCK), 1)
    return jnp.where((row < rows) & (col < cols), block.astype(jnp.float32), 0.0).astype(jnp.bfloat16)


def loaded_kernel(sizes_hbm, cur_hbm, tensors_hbm, couplings_hbm, pattern_hbm, *refs):
    parcel_ref, even_ref, head_ref, tail_ref, weights_ref, sizes_ref, tensors_ref, pattern_ref, sems = refs
    copies = [
        pltpu.make_async_copy(source, target, sems.at[at])
        for at, (source, target) in enumerate(
            (
                (sizes_hbm, sizes_ref),
                (tensors_hbm, tensors_ref),
                (couplings_hbm, weights_ref),
                (pattern_hbm, pattern_ref),
                (cur_hbm, parcel_ref.at[:CHANNELS]),
                (cur_hbm.at[:HEAD], head_ref),
                (cur_hbm.at[HEAD:], tail_ref.at[:TAIL]),
            )
        )
    ]
    for copy in copies:
        copy.start()
    copies[0].wait()
    copies[1].wait()
    sector = lax.axis_index("sec")
    for state in range(STATES):
        target = jnp.minimum(sector + state // 2 * CHARGES + state % 2, SECTORS - 1)
        block = masked(tensors_ref[state], sizes_ref[sector], sizes_ref[target])
        if state % 2:
            parcel_ref[CHANNELS + state // 2] = block
            tail_ref[TAIL + state // 2] = block
        else:
            even_ref[state // 2] = block
    copies[2].wait()
    copies[3].wait()
    pattern = pattern_ref[...].astype(jnp.float32)
    for state in range(STATES):
        weights_ref[state] = weights_ref[state] * pattern
    for copy in copies[4:]:
        copy.wait()


COSTS = dict(
    loaded=1, first=1, own_2=0.01, own_0=0.01, kept=1,
    **{f"{kind}_{low}": 10 if low < CUTS[-2] else 1 for kind in ("total", "placed") for low in CUTS},
    **{f"sent_{low}": 1 if low else 10 for low in CUTS},
)


def cost(name):
    return pl.CostEstimate(flops=int(COSTS[name] * 2.5e9), bytes_accessed=1 << 20, transcendentals=0)


def loaded(sizes, cur, tensors, couplings, pattern):
    stay = [pltpu.with_memory_space_constraint(x, pltpu.HBM) for x in (sizes, cur, tensors, couplings, pattern)]
    return pl.pallas_call(
        loaded_kernel,
        out_shape=(
            array(jnp.bfloat16, CHANNELS + 2, BLOCK, BLOCK),
            array(jnp.bfloat16, 2, BLOCK, BLOCK),
            array(jnp.bfloat16, HEAD, BLOCK, BLOCK),
            array(jnp.bfloat16, TAIL + 2, BLOCK, BLOCK),
            array(jnp.float32, STATES, CHANNELS, CHANNELS),
        ),
        in_specs=[HBM] * 5,
        out_specs=(VMEM,) * 5,
        scratch_shapes=[
            pltpu.SMEM((SECTORS,), jnp.int32),
            pltpu.VMEM((STATES, BLOCK, BLOCK), jnp.bfloat16),
            pltpu.VMEM((CHANNELS, CHANNELS), jnp.int32),
            pltpu.SemaphoreType.DMA((7,)),
        ],
        compiler_params=PARAMS,
        cost_estimate=cost("loaded"),
        name="loaded",
    )(*stay)


def first_kernel(parcel_ref, weights_ref, out_ref, mixed_ref):
    def emit(c, value):
        out_ref[c] = value.astype(out_ref.dtype)

    low, high = CHUNKS[0]
    spread = spread_weights(weights_ref[3], low, high)
    update([parcel_ref.at[:CHANNELS]], parcel_ref[CHANNELS + 1], spread, high - low, mixed_ref, emit)


def first(parcel, weights):
    low, high = CHUNKS[0]
    return pl.pallas_call(
        first_kernel,
        out_shape=array(jnp.bfloat16, high - low, BLOCK, BLOCK),
        in_specs=[VMEM] * 2,
        out_specs=VMEM,
        scratch_shapes=[MIXED],
        compiler_params=PARAMS,
        cost_estimate=cost("first"),
        name="first",
    )(parcel, weights)


def own_kernel(state, again, cur_ref, even_ref, weights_ref, _, out_ref, spread_ref, *refs):
    *later_refs, mixed_ref, sem = refs

    def emit(c, value):
        out_ref[c] = value

    copies = [pltpu.make_async_copy(cur_ref, ref, sem) for ref in later_refs]
    for copy in copies:
        copy.start()
    spread = spread_weights(weights_ref[state], 0, CHANNELS)
    update([cur_ref.at[:CHANNELS]], even_ref[state // 2], spread, CHANNELS, mixed_ref, emit)
    spread_ref[...] = spread_weights(weights_ref[state + 1], 0, CHANNELS)
    for copy in copies:
        copy.wait()


def own(state, again, cur, even, weights, after):
    name = f"own_{state}"
    return pl.pallas_call(
        functools.partial(own_kernel, state, again),
        out_shape=(
            array(jnp.float32, CHANNELS, BLOCK, BLOCK),
            array(jnp.bfloat16, ROWS, 2 * ROWS),
            *(array(cur.dtype, *cur.shape),) * again,
        ),
        in_specs=[VMEM] * 3 + [ANY],
        out_specs=(VMEM,) * (2 + again),
        scratch_shapes=[MIXED, pltpu.SemaphoreType.DMA],
        compiler_params=PARAMS,
        cost_estimate=cost(name),
        name=name,
    )(cur, even, weights, after)


def joined_kernel(state, low, high, came, base_ref, spread_ref, head_ref, tail_ref, plain_ref, _, out_ref, mixed_ref):
    carried = lax.rem(lax.axis_index("sec"), CHARGES) == CARRY + 1

    def work_out(cur_refs, block):
        def emit(c, value):
            out_ref[c] = (base_ref[low + c] + value).astype(out_ref.dtype)

        update(cur_refs, block, spread_ref[low * TILE : high * TILE, :], high - low, mixed_ref, emit)

    @pl.when(carried)
    def _():
        work_out([head_ref, tail_ref.at[:TAIL]], tail_ref[TAIL + state // 2])

    @pl.when(jnp.logical_not(carried))
    def _():
        if came:
            out_ref[...] = (base_ref[low:high] + plain_ref[...].astype(jnp.float32)).astype(out_ref.dtype)
        else:
            work_out([plain_ref.at[:CHANNELS]], plain_ref[CHANNELS + state // 2])


def joined(name, state, low, high, came, dtype, base, spread, head, tail, plain, after):
    return pl.pallas_call(
        functools.partial(joined_kernel, state, low, high, came),
        out_shape=array(dtype, high - low, BLOCK, BLOCK),
        in_specs=[VMEM] * 5 + [ANY],
        out_specs=VMEM,
        scratch_shapes=[MIXED],
        compiler_params=PARAMS,
        cost_estimate=cost(name),
        name=name,
    )(base, spread, head, tail, plain, after)


def total_kernel(low, kept_ref, *refs):
    *part_refs, _, out_ref = refs
    at = 0
    for part_ref in part_refs:
        end = at + part_ref.shape[0]
        out_ref[at:end] = (kept_ref[low + at : low + end] + part_ref[...].astype(jnp.float32)).astype(jnp.bfloat16)
        at = end


def total(low, high, kept, parts, after):
    return pl.pallas_call(
        functools.partial(total_kernel, low),
        out_shape=array(jnp.bfloat16, high - low, BLOCK, BLOCK),
        in_specs=[VMEM] * (1 + len(parts)) + [ANY],
        out_specs=VMEM,
        compiler_params=PARAMS,
        cost_estimate=cost(f"total_{low}"),
        name=f"total_{low}",
    )(kept, *parts, after)


def placed_kernel(low, high, done_ref, came_ref, *refs):
    whole_hbm, handed_hbm, sems = refs[-3:]
    copies = [
        pltpu.make_async_copy(done_ref, whole_hbm.at[low:high], sems.at[0]),
        pltpu.make_async_copy(came_ref, handed_hbm.at[low:high], sems.at[1]),
    ]
    for copy in copies:
        copy.start()
    for copy in copies:
        copy.wait()


def placed(wholes, low, high, done, came):
    whole = array(done.dtype, CHANNELS, BLOCK, BLOCK)
    return pl.pallas_call(
        functools.partial(placed_kernel, low, high),
        out_shape=(whole, whole),
        in_specs=[VMEM] * 2 + [HBM] * len(wholes),
        out_specs=(HBM, HBM),
        scratch_shapes=[pltpu.SemaphoreType.DMA((2,))],
        input_output_aliases={2: 0, 3: 1} if wholes else {},
        compiler_params=PARAMS,
        cost_estimate=cost(f"placed_{low}"),
        name=f"placed_{low}",
    )(done, came, *wholes)


def per_device(site_tensors, boundary, couplings, pattern, sizes):
    parcel, even, head, tail, weights = loaded(sizes, boundary[0, 0], site_tensors[0, 0], couplings[0], pattern)
    head = send(head, "sec", 1, (CARRY,))
    tail = send(tail, "sec", -CARRY, (CARRY,))
    tail = send(tail, "sec", CARRY + 1, (0,))
    sent = first(parcel, weights)
    came = send(sent, "sec", 1, PLAIN)
    up, spread_up, later = own(2, 1, parcel, even, weights, sent)
    plain = send(later, "sec", 1, PLAIN)
    kept, spread_kept = own(0, 0, parcel, even, weights, up)
    arrived, last = [], kept
    for low, high in CHUNKS:
        here = plain if low else came
        last = joined(f"sent_{low}", 3, low, high, not low, jnp.bfloat16, up, spread_up, head, tail, here, last)
        arrived.append(send(last, "sec", CHARGES))
    kept = last = joined("kept", 1, 0, CHANNELS, False, jnp.float32, kept, spread_kept, head, tail, plain, last)
    waiting, wholes = [], ()
    for chunks in HANDED:
        low, high = CUTS[chunks[0]], CUTS[chunks[-1] + 1]
        last = total(low, high, kept, [arrived[at] for at in chunks], last)
        waiting.append((low, high, last, send(last, "seg", 1)))
    for parts in waiting:
        wholes = placed(wholes, *parts)
    return tuple(whole[None, None] for whole in wholes)


def solution(mesh):
    return jax.shard_map(
        per_device,
        mesh=mesh,
        in_specs=(
            P("seg", "sec", None, None, None),
            P("seg", "sec", None, None, None),
            P("seg", None, None, None),
            P(),
            P(),
        ),
        out_specs=(P("seg", "sec", None, None, None), P("seg", "sec", None, None, None)),
        check_vma=False,
    )
```

```python
import functools

import jax
import jax.numpy as jnp
from jax import lax
from jax.experimental import pallas as pl
from jax.experimental.pallas import tpu as pltpu
from jax.sharding import PartitionSpec as P

STATES = 4
CHARGES = 8
BLOCK = 128
CHANNELS = 24
SECTORS = 64
TILE = 16
ROWS = CHANNELS * TILE
CARRY = 3
PLAIN = (0, 1, 2, 4, 5, 6)
HEAD = 18
TAIL = CHANNELS - HEAD
CUTS = (0, 12, 18, 24)
HANDED = ((0,), (1,), (2,))
CHUNKS = tuple(zip(CUTS[:-1], CUTS[1:]))
VMEM = pl.BlockSpec(memory_space=pltpu.VMEM)
SMEM = pl.BlockSpec(memory_space=pltpu.SMEM)
HBM = pl.BlockSpec(memory_space=pltpu.HBM)
ANY = pl.BlockSpec(memory_space=pl.ANY)
PARAMS = pltpu.CompilerParams(vmem_limit_bytes=32 * 1024 * 1024)
MIXED = pltpu.VMEM((CHANNELS, BLOCK, BLOCK), jnp.bfloat16)


def array(dtype, *shape):
    return jax.ShapeDtypeStruct(shape, dtype)


def send(shard, axis, by, charges=range(CHARGES)):
    devices = lax.axis_size(axis)
    pairs = [(i, i + by) for i in range(devices) if 0 <= i + by < devices]
    if axis == "sec":
        pairs = [(i, j) for i, j in pairs if i % CHARGES in charges]
    return lax.ppermute(shard, axis, pairs)


def two_terms(x):
    high = x.astype(jnp.bfloat16)
    low = (x - high.astype(jnp.float32)).astype(jnp.bfloat16)
    return high, low


def spread_weights(weights, low, high):
    rows = (high - low) * TILE
    channel_of_row = lax.broadcasted_iota(jnp.int32, (rows, CHANNELS), 0) // TILE + low
    pick_c = (channel_of_row == lax.broadcasted_iota(jnp.int32, (rows, CHANNELS), 1)).astype(jnp.bfloat16)
    channel_of_row = lax.broadcasted_iota(jnp.int32, (ROWS, CHANNELS), 0) // TILE
    pick_b = (channel_of_row == lax.broadcasted_iota(jnp.int32, (ROWS, CHANNELS), 1)).astype(jnp.bfloat16)
    row = lax.broadcasted_iota(jnp.int32, (rows, ROWS), 0) % TILE
    col = lax.broadcasted_iota(jnp.int32, (rows, ROWS), 1) % TILE
    same = row == col
    contract = (((1,), (1,)), ((), ()))
    parts = []
    for term in two_terms(weights):
        by_row = lax.dot_general(pick_c, term, contract, preferred_element_type=jnp.float32)
        full = lax.dot_general(by_row.astype(jnp.bfloat16), pick_b, contract, preferred_element_type=jnp.float32)
        parts.append(jnp.where(same, full, 0.0).astype(jnp.bfloat16))
    return jnp.concatenate(parts, axis=1)


def update(cur_refs, block, spread, count, mixed_ref, emit):
    def rows_at(at):
        parts = [ref[:, at : at + TILE, :].reshape(ref.shape[0] * TILE, BLOCK) for ref in cur_refs]
        return parts[0] if len(parts) == 1 else jnp.concatenate(parts, axis=0)

    for first in range(0, BLOCK, 2 * TILE):
        left, right = rows_at(first), rows_at(first + TILE)
        both = jnp.concatenate([left, right], axis=1)
        both = jnp.concatenate([both, both], axis=0)
        mixed = jnp.dot(spread, both, preferred_element_type=jnp.float32).astype(jnp.bfloat16)
        for half in range(2):
            at = first + half * TILE
            mixed_ref[:count, at : at + TILE, :] = mixed[:, half * BLOCK : (half + 1) * BLOCK].reshape(count, TILE, BLOCK)
    left_block = block.astype(jnp.float32).T.astype(jnp.bfloat16)
    left_block = jnp.concatenate([left_block, left_block], axis=1)
    for c in range(0, count, 2):
        rows = mixed_ref[c : c + 2].reshape(2 * BLOCK, BLOCK)
        high, low = two_terms(jnp.dot(rows, block, preferred_element_type=jnp.float32))
        first = jnp.concatenate([high[:BLOCK], high[BLOCK:]], axis=1)
        second = jnp.concatenate([low[:BLOCK], low[BLOCK:]], axis=1)
        pairs = jnp.concatenate([first, second], axis=0)
        result = jnp.dot(left_block, pairs, preferred_element_type=jnp.float32)
        emit(c, result[:, :BLOCK])
        emit(c + 1, result[:, BLOCK:])


def masked(block, rows, cols):
    row = lax.broadcasted_iota(jnp.int32, (BLOCK, BLOCK), 0)
    col = lax.broadcasted_iota(jnp.int32, (BLOCK, BLOCK), 1)
    return jnp.where((row < rows) & (col < cols), block.astype(jnp.float32), 0.0).astype(jnp.bfloat16)


def loaded_kernel(sizes_hbm, cur_hbm, tensors_hbm, couplings_hbm, pattern_hbm, *refs):
    parcel_ref, even_ref, head_ref, tail_ref, weights_ref, sizes_ref, tensors_ref, pattern_ref, sems = refs
    copies = [
        pltpu.make_async_copy(source, target, sems.at[at])
        for at, (source, target) in enumerate(
            (
                (sizes_hbm, sizes_ref),
                (tensors_hbm, tensors_ref),
                (couplings_hbm, weights_ref),
                (pattern_hbm, pattern_ref),
                (cur_hbm, parcel_ref.at[:CHANNELS]),
                (cur_hbm.at[:HEAD], head_ref),
                (cur_hbm.at[HEAD:], tail_ref.at[:TAIL]),
            )
        )
    ]
    for copy in copies:
        copy.start()
    copies[0].wait()
    copies[1].wait()
    sector = lax.axis_index("sec")
    for state in range(STATES):
        target = jnp.minimum(sector + state // 2 * CHARGES + state % 2, SECTORS - 1)
        block = masked(tensors_ref[state], sizes_ref[sector], sizes_ref[target])
        if state % 2:
            parcel_ref[CHANNELS + state // 2] = block
            tail_ref[TAIL + state // 2] = block
        else:
            even_ref[state // 2] = block
    copies[2].wait()
    copies[3].wait()
    pattern = pattern_ref[...].astype(jnp.float32)
    for state in range(STATES):
        weights_ref[state] = weights_ref[state] * pattern
    for copy in copies[4:]:
        copy.wait()


COSTS = dict(
    loaded=1, first=1, own_2=0.01, own_0=0.01, kept=1,
    **{f"{kind}_{low}": 10 if low < CUTS[-2] else 1 for kind in ("total", "placed") for low in CUTS},
    **{f"sent_{low}": 1 if low else 10 for low in CUTS},
)


def cost(name):
    return pl.CostEstimate(flops=int(COSTS[name] * 2.5e9), bytes_accessed=1 << 20, transcendentals=0)


def loaded(sizes, cur, tensors, couplings, pattern):
    stay = [pltpu.with_memory_space_constraint(x, pltpu.HBM) for x in (sizes, cur, tensors, couplings, pattern)]
    return pl.pallas_call(
        loaded_kernel,
        out_shape=(
            array(jnp.bfloat16, CHANNELS + 2, BLOCK, BLOCK),
            array(jnp.bfloat16, 2, BLOCK, BLOCK),
            array(jnp.bfloat16, HEAD, BLOCK, BLOCK),
            array(jnp.bfloat16, TAIL + 2, BLOCK, BLOCK),
            array(jnp.float32, STATES, CHANNELS, CHANNELS),
        ),
        in_specs=[HBM] * 5,
        out_specs=(VMEM,) * 5,
        scratch_shapes=[
            pltpu.SMEM((SECTORS,), jnp.int32),
            pltpu.VMEM((STATES, BLOCK, BLOCK), jnp.bfloat16),
            pltpu.VMEM((CHANNELS, CHANNELS), jnp.int32),
            pltpu.SemaphoreType.DMA((7,)),
        ],
        compiler_params=PARAMS,
        cost_estimate=cost("loaded"),
        name="loaded",
    )(*stay)


def first_kernel(parcel_ref, weights_ref, out_ref, mixed_ref):
    def emit(c, value):
        out_ref[c] = value.astype(out_ref.dtype)

    low, high = CHUNKS[0]
    spread = spread_weights(weights_ref[3], low, high)
    update([parcel_ref.at[:CHANNELS]], parcel_ref[CHANNELS + 1], spread, high - low, mixed_ref, emit)


def first(parcel, weights):
    low, high = CHUNKS[0]
    return pl.pallas_call(
        first_kernel,
        out_shape=array(jnp.bfloat16, high - low, BLOCK, BLOCK),
        in_specs=[VMEM] * 2,
        out_specs=VMEM,
        scratch_shapes=[MIXED],
        compiler_params=PARAMS,
        cost_estimate=cost("first"),
        name="first",
    )(parcel, weights)


def own_kernel(state, again, cur_ref, even_ref, weights_ref, _, out_ref, spread_ref, *refs):
    *later_refs, mixed_ref, sem = refs

    def emit(c, value):
        out_ref[c] = value

    copies = [pltpu.make_async_copy(cur_ref, ref, sem) for ref in later_refs]
    for copy in copies:
        copy.start()
    spread = spread_weights(weights_ref[state], 0, CHANNELS)
    update([cur_ref.at[:CHANNELS]], even_ref[state // 2], spread, CHANNELS, mixed_ref, emit)
    spread_ref[...] = spread_weights(weights_ref[state + 1], 0, CHANNELS)
    for copy in copies:
        copy.wait()


def own(state, again, cur, even, weights, after):
    name = f"own_{state}"
    return pl.pallas_call(
        functools.partial(own_kernel, state, again),
        out_shape=(
            array(jnp.float32, CHANNELS, BLOCK, BLOCK),
            array(jnp.bfloat16, ROWS, 2 * ROWS),
            *(array(cur.dtype, *cur.shape),) * again,
        ),
        in_specs=[VMEM] * 3 + [ANY],
        out_specs=(VMEM,) * (2 + again),
        scratch_shapes=[MIXED, pltpu.SemaphoreType.DMA],
        compiler_params=PARAMS,
        cost_estimate=cost(name),
        name=name,
    )(cur, even, weights, after)


def joined_kernel(state, low, high, came, base_ref, spread_ref, head_ref, tail_ref, plain_ref, _, out_ref, mixed_ref):
    carried = lax.rem(lax.axis_index("sec"), CHARGES) == CARRY + 1

    def work_out(cur_refs, block):
        def emit(c, value):
            out_ref[c] = (base_ref[low + c] + value).astype(out_ref.dtype)

        update(cur_refs, block, spread_ref[low * TILE : high * TILE, :], high - low, mixed_ref, emit)

    @pl.when(carried)
    def _():
        work_out([head_ref, tail_ref.at[:TAIL]], tail_ref[TAIL + state // 2])

    @pl.when(jnp.logical_not(carried))
    def _():
        if came:
            out_ref[...] = (base_ref[low:high] + plain_ref[...].astype(jnp.float32)).astype(out_ref.dtype)
        else:
            work_out([plain_ref.at[:CHANNELS]], plain_ref[CHANNELS + state // 2])


def joined(name, state, low, high, came, dtype, base, spread, head, tail, plain, after):
    return pl.pallas_call(
        functools.partial(joined_kernel, state, low, high, came),
        out_shape=array(dtype, high - low, BLOCK, BLOCK),
        in_specs=[VMEM] * 5 + [ANY],
        out_specs=VMEM,
        scratch_shapes=[MIXED],
        compiler_params=PARAMS,
        cost_estimate=cost(name),
        name=name,
    )(base, spread, head, tail, plain, after)


def total_kernel(low, kept_ref, *refs):
    *part_refs, _, out_ref = refs
    at = 0
    for part_ref in part_refs:
        end = at + part_ref.shape[0]
        out_ref[at:end] = (kept_ref[low + at : low + end] + part_ref[...].astype(jnp.float32)).astype(jnp.bfloat16)
        at = end


def total(low, high, kept, parts, after):
    return pl.pallas_call(
        functools.partial(total_kernel, low),
        out_shape=array(jnp.bfloat16, high - low, BLOCK, BLOCK),
        in_specs=[VMEM] * (1 + len(parts)) + [ANY],
        out_specs=VMEM,
        compiler_params=PARAMS,
        cost_estimate=cost(f"total_{low}"),
        name=f"total_{low}",
    )(kept, *parts, after)


def placed_kernel(low, high, done_ref, came_ref, *refs):
    whole_hbm, handed_hbm, sems = refs[-3:]
    copies = [
        pltpu.make_async_copy(done_ref, whole_hbm.at[low:high], sems.at[0]),
        pltpu.make_async_copy(came_ref, handed_hbm.at[low:high], sems.at[1]),
    ]
    for copy in copies:
        copy.start()
    for copy in copies:
        copy.wait()


def placed(wholes, low, high, done, came):
    whole = array(done.dtype, CHANNELS, BLOCK, BLOCK)
    return pl.pallas_call(
        functools.partial(placed_kernel, low, high),
        out_shape=(whole, whole),
        in_specs=[VMEM] * 2 + [HBM] * len(wholes),
        out_specs=(HBM, HBM),
        scratch_shapes=[pltpu.SemaphoreType.DMA((2,))],
        input_output_aliases={2: 0, 3: 1} if wholes else {},
        compiler_params=PARAMS,
        cost_estimate=cost(f"placed_{low}"),
        name=f"placed_{low}",
    )(done, came, *wholes)


def per_device(site_tensors, boundary, couplings, pattern, sizes):
    parcel, even, head, tail, weights = loaded(sizes, boundary[0, 0], site_tensors[0, 0], couplings[0], pattern)
    head = send(head, "sec", 1, (CARRY,))
    tail = send(tail, "sec", -CARRY, (CARRY,))
    tail = send(tail, "sec", CARRY + 1, (0,))
    sent = first(parcel, weights)
    came = send(sent, "sec", 1, PLAIN)
    up, spread_up, later = own(2, 1, parcel, even, weights, sent)
    plain = send(later, "sec", 1, PLAIN)
    kept, spread_kept = own(0, 0, parcel, even, weights, up)
    arrived, last = [], kept
    for low, high in CHUNKS:
        here = plain if low else came
        last = joined(f"sent_{low}", 3, low, high, not low, jnp.bfloat16, up, spread_up, head, tail, here, last)
        arrived.append(send(last, "sec", CHARGES))
    kept = last = joined("kept", 1, 0, CHANNELS, False, jnp.float32, kept, spread_kept, head, tail, plain, last)
    waiting, wholes = [], ()
    for chunks in HANDED:
        low, high = CUTS[chunks[0]], CUTS[chunks[-1] + 1]
        last = total(low, high, kept, [arrived[at] for at in chunks], last)
        waiting.append((low, high, last, send(last, "seg", 1)))
    for parts in waiting:
        wholes = placed(wholes, *parts)
    return tuple(whole[None, None] for whole in wholes)


def solution(mesh):
    return jax.shard_map(
        per_device,
        mesh=mesh,
        in_specs=(
            P("seg", "sec", None, None, None),
            P("seg", "sec", None, None, None),
            P("seg", None, None, None),
            P(),
            P(),
        ),
        out_specs=(P("seg", "sec", None, None, None), P("seg", "sec", None, None, None)),
        check_vma=False,
    )
```

```python
import functools

import jax
import jax.numpy as jnp
from jax import lax
from jax.experimental import pallas as pl
from jax.experimental.pallas import tpu as pltpu
from jax.sharding import PartitionSpec as P

STATES = 4
CHARGES = 8
BLOCK = 128
CHANNELS = 24
SECTORS = 64
TILE = 16
ROWS = CHANNELS * TILE
CARRY = 3
PLAIN = (0, 1, 2, 4, 5, 6)
HEAD = 16
TAIL = CHANNELS - HEAD
CUTS = (0, 12, 18, 24)
HANDED = ((0,), (1,), (2,))
CHUNKS = tuple(zip(CUTS[:-1], CUTS[1:]))
VMEM = pl.BlockSpec(memory_space=pltpu.VMEM)
SMEM = pl.BlockSpec(memory_space=pltpu.SMEM)
HBM = pl.BlockSpec(memory_space=pltpu.HBM)
ANY = pl.BlockSpec(memory_space=pl.ANY)
PARAMS = pltpu.CompilerParams(vmem_limit_bytes=32 * 1024 * 1024)
MIXED = pltpu.VMEM((CHANNELS, BLOCK, BLOCK), jnp.bfloat16)


def array(dtype, *shape):
    return jax.ShapeDtypeStruct(shape, dtype)


def send(shard, axis, by, charges=range(CHARGES)):
    devices = lax.axis_size(axis)
    pairs = [(i, i + by) for i in range(devices) if 0 <= i + by < devices]
    if axis == "sec":
        pairs = [(i, j) for i, j in pairs if i % CHARGES in charges]
    return lax.ppermute(shard, axis, pairs)


def two_terms(x):
    high = x.astype(jnp.bfloat16)
    low = (x - high.astype(jnp.float32)).astype(jnp.bfloat16)
    return high, low


def spread_weights(weights, low, high):
    rows = (high - low) * TILE
    channel_of_row = lax.broadcasted_iota(jnp.int32, (rows, CHANNELS), 0) // TILE + low
    pick_c = (channel_of_row == lax.broadcasted_iota(jnp.int32, (rows, CHANNELS), 1)).astype(jnp.bfloat16)
    channel_of_row = lax.broadcasted_iota(jnp.int32, (ROWS, CHANNELS), 0) // TILE
    pick_b = (channel_of_row == lax.broadcasted_iota(jnp.int32, (ROWS, CHANNELS), 1)).astype(jnp.bfloat16)
    row = lax.broadcasted_iota(jnp.int32, (rows, ROWS), 0) % TILE
    col = lax.broadcasted_iota(jnp.int32, (rows, ROWS), 1) % TILE
    same = row == col
    contract = (((1,), (1,)), ((), ()))
    parts = []
    for term in two_terms(weights):
        by_row = lax.dot_general(pick_c, term, contract, preferred_element_type=jnp.float32)
        full = lax.dot_general(by_row.astype(jnp.bfloat16), pick_b, contract, preferred_element_type=jnp.float32)
        parts.append(jnp.where(same, full, 0.0).astype(jnp.bfloat16))
    return jnp.concatenate(parts, axis=1)


def update(cur_refs, block, spread, count, mixed_ref, emit):
    def rows_at(at):
        parts = [ref[:, at : at + TILE, :].reshape(ref.shape[0] * TILE, BLOCK) for ref in cur_refs]
        return parts[0] if len(parts) == 1 else jnp.concatenate(parts, axis=0)

    for first in range(0, BLOCK, 2 * TILE):
        left, right = rows_at(first), rows_at(first + TILE)
        both = jnp.concatenate([left, right], axis=1)
        both = jnp.concatenate([both, both], axis=0)
        mixed = jnp.dot(spread, both, preferred_element_type=jnp.float32).astype(jnp.bfloat16)
        for half in range(2):
            at = first + half * TILE
            mixed_ref[:count, at : at + TILE, :] = mixed[:, half * BLOCK : (half + 1) * BLOCK].reshape(count, TILE, BLOCK)
    left_block = block.astype(jnp.float32).T.astype(jnp.bfloat16)
    left_block = jnp.concatenate([left_block, left_block], axis=1)
    for c in range(0, count, 2):
        rows = mixed_ref[c : c + 2].reshape(2 * BLOCK, BLOCK)
        high, low = two_terms(jnp.dot(rows, block, preferred_element_type=jnp.float32))
        first = jnp.concatenate([high[:BLOCK], high[BLOCK:]], axis=1)
        second = jnp.concatenate([low[:BLOCK], low[BLOCK:]], axis=1)
        pairs = jnp.concatenate([first, second], axis=0)
        result = jnp.dot(left_block, pairs, preferred_element_type=jnp.float32)
        emit(c, result[:, :BLOCK])
        emit(c + 1, result[:, BLOCK:])


def masked(block, rows, cols):
    row = lax.broadcasted_iota(jnp.int32, (BLOCK, BLOCK), 0)
    col = lax.broadcasted_iota(jnp.int32, (BLOCK, BLOCK), 1)
    return jnp.where((row < rows) & (col < cols), block.astype(jnp.float32), 0.0).astype(jnp.bfloat16)


def loaded_kernel(sizes_hbm, cur_hbm, tensors_hbm, couplings_hbm, pattern_hbm, *refs):
    parcel_ref, even_ref, head_ref, tail_ref, weights_ref, sizes_ref, tensors_ref, pattern_ref, sems = refs
    copies = [
        pltpu.make_async_copy(source, target, sems.at[at])
        for at, (source, target) in enumerate(
            (
                (sizes_hbm, sizes_ref),
                (tensors_hbm, tensors_ref),
                (couplings_hbm, weights_ref),
                (pattern_hbm, pattern_ref),
                (cur_hbm, parcel_ref.at[:CHANNELS]),
                (cur_hbm.at[:HEAD], head_ref),
                (cur_hbm.at[HEAD:], tail_ref.at[:TAIL]),
            )
        )
    ]
    for copy in copies:
        copy.start()
    copies[0].wait()
    copies[1].wait()
    sector = lax.axis_index("sec")
    for state in range(STATES):
        target = jnp.minimum(sector + state // 2 * CHARGES + state % 2, SECTORS - 1)
        block = masked(tensors_ref[state], sizes_ref[sector], sizes_ref[target])
        if state % 2:
            parcel_ref[CHANNELS + state // 2] = block
            tail_ref[TAIL + state // 2] = block
        else:
            even_ref[state // 2] = block
    copies[2].wait()
    copies[3].wait()
    pattern = pattern_ref[...].astype(jnp.float32)
    for state in range(STATES):
        weights_ref[state] = weights_ref[state] * pattern
    for copy in copies[4:]:
        copy.wait()


COSTS = dict(
    loaded=1, first=1, own_2=0.01, own_0=0.01, kept=1,
    **{f"{kind}_{low}": 10 if low < CUTS[-2] else 1 for kind in ("total", "placed") for low in CUTS},
    **{f"sent_{low}": 1 if low else 10 for low in CUTS},
)


def cost(name):
    return pl.CostEstimate(flops=int(COSTS[name] * 2.5e9), bytes_accessed=1 << 20, transcendentals=0)


def loaded(sizes, cur, tensors, couplings, pattern):
    stay = [pltpu.with_memory_space_constraint(x, pltpu.HBM) for x in (sizes, cur, tensors, couplings, pattern)]
    return pl.pallas_call(
        loaded_kernel,
        out_shape=(
            array(jnp.bfloat16, CHANNELS + 2, BLOCK, BLOCK),
            array(jnp.bfloat16, 2, BLOCK, BLOCK),
            array(jnp.bfloat16, HEAD, BLOCK, BLOCK),
            array(jnp.bfloat16, TAIL + 2, BLOCK, BLOCK),
            array(jnp.float32, STATES, CHANNELS, CHANNELS),
        ),
        in_specs=[HBM] * 5,
        out_specs=(VMEM,) * 5,
        scratch_shapes=[
            pltpu.SMEM((SECTORS,), jnp.int32),
            pltpu.VMEM((STATES, BLOCK, BLOCK), jnp.bfloat16),
            pltpu.VMEM((CHANNELS, CHANNELS), jnp.int32),
            pltpu.SemaphoreType.DMA((7,)),
        ],
        compiler_params=PARAMS,
        cost_estimate=cost("loaded"),
        name="loaded",
    )(*stay)


def first_kernel(parcel_ref, weights_ref, out_ref, mixed_ref):
    def emit(c, value):
        out_ref[c] = value.astype(out_ref.dtype)

    low, high = CHUNKS[0]
    spread = spread_weights(weights_ref[3], low, high)
    update([parcel_ref.at[:CHANNELS]], parcel_ref[CHANNELS + 1], spread, high - low, mixed_ref, emit)


def first(parcel, weights):
    low, high = CHUNKS[0]
    return pl.pallas_call(
        first_kernel,
        out_shape=array(jnp.bfloat16, high - low, BLOCK, BLOCK),
        in_specs=[VMEM] * 2,
        out_specs=VMEM,
        scratch_shapes=[MIXED],
        compiler_params=PARAMS,
        cost_estimate=cost("first"),
        name="first",
    )(parcel, weights)


def own_kernel(state, again, cur_ref, even_ref, weights_ref, _, out_ref, spread_ref, *refs):
    *later_refs, mixed_ref, sem = refs

    def emit(c, value):
        out_ref[c] = value

    copies = [pltpu.make_async_copy(cur_ref, ref, sem) for ref in later_refs]
    for copy in copies:
        copy.start()
    spread = spread_weights(weights_ref[state], 0, CHANNELS)
    update([cur_ref.at[:CHANNELS]], even_ref[state // 2], spread, CHANNELS, mixed_ref, emit)
    spread_ref[...] = spread_weights(weights_ref[state + 1], 0, CHANNELS)
    for copy in copies:
        copy.wait()


def own(state, again, cur, even, weights, after):
    name = f"own_{state}"
    return pl.pallas_call(
        functools.partial(own_kernel, state, again),
        out_shape=(
            array(jnp.float32, CHANNELS, BLOCK, BLOCK),
            array(jnp.bfloat16, ROWS, 2 * ROWS),
            *(array(cur.dtype, *cur.shape),) * again,
        ),
        in_specs=[VMEM] * 3 + [ANY],
        out_specs=(VMEM,) * (2 + again),
        scratch_shapes=[MIXED, pltpu.SemaphoreType.DMA],
        compiler_params=PARAMS,
        cost_estimate=cost(name),
        name=name,
    )(cur, even, weights, after)


def joined_kernel(state, low, high, came, base_ref, spread_ref, head_ref, tail_ref, plain_ref, _, out_ref, mixed_ref):
    carried = lax.rem(lax.axis_index("sec"), CHARGES) == CARRY + 1

    def work_out(cur_refs, block):
        def emit(c, value):
            out_ref[c] = (base_ref[low + c] + value).astype(out_ref.dtype)

        update(cur_refs, block, spread_ref[low * TILE : high * TILE, :], high - low, mixed_ref, emit)

    @pl.when(carried)
    def _():
        work_out([head_ref, tail_ref.at[:TAIL]], tail_ref[TAIL + state // 2])

    @pl.when(jnp.logical_not(carried))
    def _():
        if came:
            out_ref[...] = (base_ref[low:high] + plain_ref[...].astype(jnp.float32)).astype(out_ref.dtype)
        else:
            work_out([plain_ref.at[:CHANNELS]], plain_ref[CHANNELS + state // 2])


def joined(name, state, low, high, came, dtype, base, spread, head, tail, plain, after):
    return pl.pallas_call(
        functools.partial(joined_kernel, state, low, high, came),
        out_shape=array(dtype, high - low, BLOCK, BLOCK),
        in_specs=[VMEM] * 5 + [ANY],
        out_specs=VMEM,
        scratch_shapes=[MIXED],
        compiler_params=PARAMS,
        cost_estimate=cost(name),
        name=name,
    )(base, spread, head, tail, plain, after)


def total_kernel(low, kept_ref, *refs):
    *part_refs, _, out_ref = refs
    at = 0
    for part_ref in part_refs:
        end = at + part_ref.shape[0]
        out_ref[at:end] = (kept_ref[low + at : low + end] + part_ref[...].astype(jnp.float32)).astype(jnp.bfloat16)
        at = end


def total(low, high, kept, parts, after):
    return pl.pallas_call(
        functools.partial(total_kernel, low),
        out_shape=array(jnp.bfloat16, high - low, BLOCK, BLOCK),
        in_specs=[VMEM] * (1 + len(parts)) + [ANY],
        out_specs=VMEM,
        compiler_params=PARAMS,
        cost_estimate=cost(f"total_{low}"),
        name=f"total_{low}",
    )(kept, *parts, after)


def placed_kernel(low, high, done_ref, came_ref, *refs):
    whole_hbm, handed_hbm, sems = refs[-3:]
    copies = [
        pltpu.make_async_copy(done_ref, whole_hbm.at[low:high], sems.at[0]),
        pltpu.make_async_copy(came_ref, handed_hbm.at[low:high], sems.at[1]),
    ]
    for copy in copies:
        copy.start()
    for copy in copies:
        copy.wait()


def placed(wholes, low, high, done, came):
    whole = array(done.dtype, CHANNELS, BLOCK, BLOCK)
    return pl.pallas_call(
        functools.partial(placed_kernel, low, high),
        out_shape=(whole, whole),
        in_specs=[VMEM] * 2 + [HBM] * len(wholes),
        out_specs=(HBM, HBM),
        scratch_shapes=[pltpu.SemaphoreType.DMA((2,))],
        input_output_aliases={2: 0, 3: 1} if wholes else {},
        compiler_params=PARAMS,
        cost_estimate=cost(f"placed_{low}"),
        name=f"placed_{low}",
    )(done, came, *wholes)


def per_device(site_tensors, boundary, couplings, pattern, sizes):
    parcel, even, head, tail, weights = loaded(sizes, boundary[0, 0], site_tensors[0, 0], couplings[0], pattern)
    head = send(head, "sec", 1, (CARRY,))
    tail = send(tail, "sec", -CARRY, (CARRY,))
    tail = send(tail, "sec", CARRY + 1, (0,))
    sent = first(parcel, weights)
    came = send(sent, "sec", 1, PLAIN)
    up, spread_up, later = own(2, 1, parcel, even, weights, sent)
    plain = send(later, "sec", 1, PLAIN)
    kept, spread_kept = own(0, 0, parcel, even, weights, up)
    arrived, last = [], kept
    for low, high in CHUNKS:
        here = plain if low else came
        last = joined(f"sent_{low}", 3, low, high, not low, jnp.bfloat16, up, spread_up, head, tail, here, last)
        arrived.append(send(last, "sec", CHARGES))
    kept = last = joined("kept", 1, 0, CHANNELS, False, jnp.float32, kept, spread_kept, head, tail, plain, last)
    waiting, wholes = [], ()
    for chunks in HANDED:
        low, high = CUTS[chunks[0]], CUTS[chunks[-1] + 1]
        last = total(low, high, kept, [arrived[at] for at in chunks], last)
        waiting.append((low, high, last, send(last, "seg", 1)))
    for parts in waiting:
        wholes = placed(wholes, *parts)
    return tuple(whole[None, None] for whole in wholes)


def solution(mesh):
    return jax.shard_map(
        per_device,
        mesh=mesh,
        in_specs=(
            P("seg", "sec", None, None, None),
            P("seg", "sec", None, None, None),
            P("seg", None, None, None),
            P(),
            P(),
        ),
        out_specs=(P("seg", "sec", None, None, None), P("seg", "sec", None, None, None)),
        check_vma=False,
    )
```
